32 devices in a mesh: dp: 2 (over y), row: 4 (over z), col: 4 (over x, core).
Axes of the slice: x: 2, y: 2, z: 4, core: 2. Of those that a mesh axis runs over, the one named last changes fastest.
Arguments:
- tokens_in: bfloat16 [8192, 1024], P('dp', ('row', 'col')), may hold values from -6 to 6
- gain_first: float32 [1024], P(('row', 'col')), may hold values from 0.5 to 1.5
- proj_gate: bfloat16 [1024, 1536], P('row', 'col'), may hold values from -0.1875 to 0.1875
- proj_inner: bfloat16 [1024, 1536], P('row', 'col'), may hold values from -0.1875 to 0.1875
- proj_step: bfloat16 [1024, 24], P('row', 'col'), may hold values from -0.1875 to 0.1875
- proj_query: bfloat16 [1024, 512], P('row', 'col'), may hold values from -0.1875 to 0.1875
- proj_state: bfloat16 [1024, 256], P('row'), may hold values from -0.1875 to 0.1875
- proj_keyval: bfloat16 [1024, 256], P('row'), may hold values from -0.1875 to 0.1875
- conv_inner: float32 [4, 1536], P(None, 'col'), may hold values from -3 to 3
- conv_state: float32 [4, 256], replicated, may hold values from -3 to 3
- step_bias: float32 [24], P('col'), may hold values from -3.5 to -0.5
- decay_log: float32 [24], P('col'), may hold values from -5 to 0.5
- skip_scale: float32 [24], P('col'), may hold values from 2 to 20
- mixer_gain: float32 [1536], P('col'), may hold values from 0.5 to 1.5
- out_mamba: bfloat16 [1536, 1024], P('col', 'row'), may hold values from -0.15625 to 0.15625
- out_attn: bfloat16 [512, 1024], P('col', 'row'), may hold values from -1 to 1
- gain_second: float32 [1024], P(('row', 'col')), may hold values from 0.5 to 1.5
- ffn_gate: bfloat16 [1024, 2048], P('row', 'col'), may hold values from -0.1875 to 0.1875
- ffn_up: bfloat16 [1024, 2048], P('row', 'col'), may hold values from -0.1875 to 0.1875
- ffn_down: bfloat16 [2048, 1024], P('col', 'row'), may hold values from -0.125 to 0.125
- out_grad: bfloat16 [8192, 1024], P('dp', ('row', 'col')), may hold values from -6 to 6
Outputs:
- block_out: bfloat16 [8192, 1024], P('dp', ('row', 'col'))
- grad_tokens: bfloat16 [8192, 1024], P('dp', ('row', 'col'))
- grad_gain_first: float32 [1024], P(('row', 'col'))
- grad_proj_gate: float32 [1024, 1536], P('row', 'col')
- grad_proj_inner: float32 [1024, 1536], P('row', 'col')
- grad_proj_step: float32 [1024, 24], P('row', 'col')
- grad_proj_query: float32 [1024, 512], P('row', 'col')
- grad_proj_state: float32 [1024, 256], P('row')
- grad_proj_keyval: float32 [1024, 256], P('row')
- grad_conv_inner: float32 [4, 1536], P(None, 'col')
- grad_conv_state: float32 [4, 256], replicated
- grad_step_bias: float32 [24], P('col')
- grad_decay_log: float32 [24], P('col')
- grad_skip_scale: float32 [24], P('col')
- grad_mixer_gain: float32 [1536], P('col')
- grad_out_mamba: float32 [1536, 1024], P('col', 'row')
- grad_out_attn: float32 [512, 1024], P('col', 'row')
- grad_gain_second: float32 [1024], P(('row', 'col'))
- grad_ffn_gate: float32 [1024, 2048], P('row', 'col')
- grad_ffn_up: float32 [1024, 2048], P('row', 'col')
- grad_ffn_down: float32 [2048, 1024], P('col', 'row')
The draws below stay inside these ranges and needn't reach their ends.
All inputs are finite; a program needn't handle non-finite values.
Results may differ from the reference program's by a relative error of at most 0.019.
Values may be sent and summed in bfloat16 or wider, within the bound.
A program may use at most 192 MiB of HBM per device.

```python
import math
import jax
import jax.numpy as jnp
from jax import lax

D = 1024
FF = 2048
HM = 24
NS = 128
KC = 4
HQ = 8
HK = 2
HD = 64
DI = 1536
SEQ_LEN = 1024
TOKENS = 8192


def block_levels(rng, dims, split, low, high):
    def one(axis_at, blocks):
        draws = jax.random.uniform(jax.random.fold_in(jax.random.fold_in(rng, 6), axis_at), (blocks,), jnp.float32, low / len(split), high / len(split))
        return jnp.repeat(jnp.exp(draws), dims[axis_at] // blocks).reshape((-1,) + (1,) * (len(dims) - axis_at - 1))

    gain = one(*split[0])
    for cut in split[1:]:
        gain = gain * one(*cut)
    return gain


def bell_draw(key, shape, spread, most, pieces=(), kind=jnp.bfloat16):
    loudness = block_levels(key, shape, pieces, -0.22, 0.18) if pieces else 1.0
    values = jax.random.normal(key, shape, jnp.float32) * spread * loudness
    return jnp.minimum(jnp.maximum(values, -most), most).astype(kind)


def setup_inputs(seed: int = 0) -> dict:
    key_of = jax.random.split(jax.random.key(seed), 22)
    tokens_in = bell_draw(key_of[0], (TOKENS, D), 1.0, 6.0, ((0, 2), (1, 16)))
    gain_first = jnp.clip(1.0 + 0.1 * jax.random.normal(key_of[1], (D,), jnp.float32), 0.5, 1.5)
    proj_gate = bell_draw(key_of[2], (D, DI), D ** -0.5, 0.1875, ((0, 4), (1, 4)))
    proj_inner = bell_draw(key_of[3], (D, DI), D ** -0.5, 0.1875, ((0, 4), (1, 4)))
    proj_step = bell_draw(key_of[4], (D, HM), D ** -0.5, 0.1875, ((0, 4), (1, 4)))
    proj_query = bell_draw(key_of[5], (D, HQ * HD), D ** -0.5, 0.1875, ((0, 4), (1, 4)))
    proj_state = bell_draw(key_of[6], (D, 2 * NS), D ** -0.5, 0.1875, ((0, 4),))
    proj_keyval = bell_draw(key_of[7], (D, 2 * HK * HD), D ** -0.5, 0.1875, ((0, 4),))
    conv_inner = bell_draw(key_of[8], (KC, DI), KC ** -0.5, 3.0, ((1, 4),), jnp.float32)
    conv_state = bell_draw(key_of[9], (KC, 2 * NS), KC ** -0.5, 3.0, (), jnp.float32)
    step_bias = jnp.clip(-3.5 + 3.0 * jax.random.uniform(key_of[10], (HM,), jnp.float32) ** block_levels(key_of[10], (HM,), ((0, 4),), -0.2, 0.2), -3.5, -0.5)
    decay_log = jnp.clip(-5.0 + 5.5 * jax.random.uniform(key_of[11], (HM,), jnp.float32) ** block_levels(key_of[11], (HM,), ((0, 4),), -0.2, 0.2), -5.0, 0.5)
    skip_scale = jnp.clip(jnp.exp(math.log(20.0) - 2.3025851 * jax.random.uniform(key_of[12], (HM,), jnp.float32) ** block_levels(key_of[12], (HM,), ((0, 4),), -0.2, 0.2)), 2.0, 20.0)
    mixer_gain = jnp.clip(1.0 + 0.1 * jax.random.normal(key_of[13], (DI,), jnp.float32), 0.5, 1.5)
    out_mamba = bell_draw(key_of[14], (DI, D), DI ** -0.5, 0.15625, ((0, 4), (1, 4)))
    out_attn = bell_draw(key_of[15], (HQ * HD, D), (HQ * HD // 16) ** -0.5, 1.0, ((0, 4), (1, 4)))
    gain_second = jnp.clip(1.0 + 0.1 * jax.random.normal(key_of[16], (D,), jnp.float32), 0.5, 1.5)
    ffn_gate = bell_draw(key_of[17], (D, FF), D ** -0.5, 0.1875, ((0, 4), (1, 4)))
    ffn_up = bell_draw(key_of[18], (D, FF), D ** -0.5, 0.1875, ((0, 4), (1, 4)))
    ffn_down = bell_draw(key_of[19], (FF, D), FF ** -0.5, 0.125, ((0, 4), (1, 4)))
    out_grad = bell_draw(key_of[20], (TOKENS, D), 1.0, 6.0, ((0, 2), (1, 16)))
    return dict(tokens_in=tokens_in, gain_first=gain_first, proj_gate=proj_gate, proj_inner=proj_inner, proj_step=proj_step, proj_query=proj_query, proj_state=proj_state, proj_keyval=proj_keyval, conv_inner=conv_inner, conv_state=conv_state, step_bias=step_bias, decay_log=decay_log, skip_scale=skip_scale, mixer_gain=mixer_gain, out_mamba=out_mamba, out_attn=out_attn, gain_second=gain_second, ffn_gate=ffn_gate, ffn_up=ffn_up, ffn_down=ffn_down, out_grad=out_grad)


EPS = 1e-06
HIGH = lax.Precision.HIGHEST

@jax.custom_vjp
def low(v):
    return lax.optimization_barrier(v.astype(jnp.bfloat16)).astype(jnp.float32)

@jax.custom_vjp
def low_back(v):
    return v

def low_keep(v):
    return (low(v), None)

def low_pass(kept, grad):
    return (grad,)

def back_keep(v):
    return (v, None)

def back_low(kept, grad):
    return (low(grad),)
low.defvjp(low_keep, low_pass)
low_back.defvjp(back_keep, back_low)

def rms_norm(values, gain_vec):
    return values * lax.rsqrt(lax.optimization_barrier(jnp.mean(values * values, axis=1, keepdims=True)) + EPS) * gain_vec

def causal_conv(signal, kernel):
    tap_count = kernel.shape[0]
    length = signal.shape[0]
    padded = jnp.concatenate([jnp.zeros((tap_count - 1, signal.shape[1]), jnp.float32), signal], axis=0)
    result = kernel[tap_count - 1] * signal
    for offset in range(tap_count - 1):
        result = result + kernel[offset] * padded[offset:offset + length]
    return result

def mixer_front(inputs, conv_inner, conv_state, step_bias, decay_log, skip_scale, key_pick, head_dim):
    inner_width = conv_inner.shape[1]
    mamba_heads = step_bias.shape[0]
    state_size = conv_state.shape[1] // 2
    query_width = key_pick.shape[0] * head_dim
    length = inputs.shape[0]
    gate_part = inputs[:, :inner_width]
    inner_part = inputs[:, inner_width:2 * inner_width]
    first_col = 2 * inner_width
    step_part = inputs[:, first_col:first_col + mamba_heads]
    first_col = first_col + mamba_heads
    query_part = inputs[:, first_col:first_col + query_width]
    first_col = first_col + query_width
    state_part = inputs[:, first_col:first_col + 2 * state_size]
    keyval_part = inputs[:, first_col + 2 * state_size:]
    positions = jnp.arange(length)
    causal = positions[:, None] >= positions[None, :]
    mixed_inner = jax.nn.silu(causal_conv(inner_part, conv_inner))
    mixed_state = jax.nn.silu(causal_conv(state_part, conv_state))
    b_matrix = mixed_state[:, :state_size]
    c_matrix = mixed_state[:, state_size:]
    step_size = jax.nn.softplus(step_part + step_bias)
    decay_sum = jnp.cumsum(step_size * -jnp.exp(decay_log), axis=0)
    spans = decay_sum.T[:, :, None] - decay_sum.T[:, None, :]
    mixing = jnp.where(causal, jnp.exp(jnp.where(causal, spans, 0.0)), 0.0)
    affinity = jnp.dot(c_matrix, b_matrix.T, precision=HIGH)
    heads_inner = mixed_inner.reshape(length, mamba_heads, -1)
    scaled_inner = heads_inner * step_size[:, :, None]
    ssm_out = jnp.einsum('hts,shp->thp', mixing * affinity[None], scaled_inner, precision=HIGH)
    ssm_out = ssm_out + skip_scale[None, :, None] * heads_inner
    gated = ssm_out.reshape(length, inner_width) * jax.nn.silu(gate_part)
    key_heads = keyval_part.shape[1] // (2 * head_dim)
    queries = query_part.reshape(length, -1, head_dim)
    keys_all = keyval_part[:, :key_heads * head_dim].reshape(length, key_heads, head_dim)
    values_all = keyval_part[:, key_heads * head_dim:].reshape(length, key_heads, head_dim)
    keys_used = jnp.take(keys_all, key_pick, axis=1)
    values_used = jnp.take(values_all, key_pick, axis=1)
    scores = jnp.einsum('thd,shd->hts', queries, keys_used, precision=HIGH) / math.sqrt(head_dim)
    scores = jnp.where(causal[None], scores, -1e+30)
    peak = lax.optimization_barrier(jnp.max(scores, axis=2, keepdims=True))
    weights = jnp.exp(scores - peak)
    weights = weights / lax.optimization_barrier(jnp.sum(weights, axis=2, keepdims=True))
    attended = jnp.einsum('hts,shd->thd', weights, values_used, precision=HIGH).reshape(length, -1)
    return (gated, attended)

def layer(tokens_in, gain_first, proj_gate, proj_inner, proj_step, proj_query, proj_state, proj_keyval, conv_inner, conv_state, step_bias, decay_log, skip_scale, mixer_gain, out_mamba, out_attn, gain_second, ffn_gate, ffn_up, ffn_down):
    kernel_in = jnp.concatenate([proj_gate, proj_inner, proj_step, proj_query, proj_state, proj_keyval], axis=1)
    normed = low(rms_norm(tokens_in, gain_first))
    mixer_in = low(low_back(jnp.dot(normed, kernel_in, precision=HIGH)))
    by_sequence = mixer_in.reshape(-1, SEQ_LEN, mixer_in.shape[1])
    key_pick = (jnp.arange(HQ) // (HQ // HK)).astype(jnp.int32)

    def front_seq(seq_in):
        return mixer_front(seq_in, conv_inner, conv_state, step_bias, decay_log, skip_scale, key_pick, HD)
    gated, attended = lax.map(jax.checkpoint(front_seq), by_sequence)
    gated = gated.reshape(-1, DI)
    attended = attended.reshape(-1, HQ * HD)
    mixed = low(jnp.concatenate([rms_norm(gated, mixer_gain), attended], axis=1))
    kernel_out = jnp.concatenate([out_mamba, out_attn], axis=0)
    hidden = tokens_in + low_back(jnp.dot(mixed, kernel_out, precision=HIGH))
    normed_two = low(rms_norm(hidden, gain_second))
    gate_val = low_back(jnp.dot(normed_two, ffn_gate, precision=HIGH))
    up_val = low_back(jnp.dot(normed_two, ffn_up, precision=HIGH))
    active = low(jax.nn.silu(gate_val) * up_val)
    return hidden + low_back(jnp.dot(active, ffn_down, precision=HIGH))

def reference(tokens_in, gain_first, proj_gate, proj_inner, proj_step, proj_query, proj_state, proj_keyval, conv_inner, conv_state, step_bias, decay_log, skip_scale, mixer_gain, out_mamba, out_attn, gain_second, ffn_gate, ffn_up, ffn_down, out_grad):
    inputs = (tokens_in, gain_first, proj_gate, proj_inner, proj_step, proj_query, proj_state, proj_keyval, conv_inner, conv_state, step_bias, decay_log, skip_scale, mixer_gain, out_mamba, out_attn, gain_second, ffn_gate, ffn_up, ffn_down)
    inputs = tuple((item.astype(jnp.float32) for item in inputs))
    result, pull = jax.vjp(layer, *inputs)
    grads = pull(out_grad.astype(jnp.float32))
    return (result.astype(jnp.bfloat16), grads[0].astype(jnp.bfloat16), grads[1], grads[2], grads[3], grads[4], grads[5], grads[6], grads[7], grads[8], grads[9], grads[10], grads[11], grads[12], grads[13], grads[14], grads[15], grads[16], grads[17], grads[18], grads[19])
```

```python
import math

import jax
import jax.numpy as jnp
from jax import lax
from jax.sharding import PartitionSpec as P

D = 1024
HQ = 8
HK = 2
HD = 64
DI = 1536
SEQ_LEN = 1024
CHUNK = 128


EPS = 1e-06
HIGH = lax.Precision.HIGHEST


def plain_dot(left, right):
    return jnp.dot(left, right, preferred_element_type=jnp.float32)


def dot_nt(left, right):
    return lax.dot_general(
        left, right, (((1,), (1,)), ((), ())), preferred_element_type=jnp.float32
    )


def dot_tn(left, right):
    return lax.dot_general(
        left, right, (((0,), (0,)), ((), ())), preferred_element_type=jnp.float32
    )


def gather_rows(weight):
    return lax.all_gather(weight, "row", axis=0, tiled=True)


def gather_tokens(values):
    return lax.all_gather(values, "col", axis=0, tiled=True)


def sum_tokens(partial_sum):
    return lax.psum_scatter(
        partial_sum.astype(jnp.bfloat16), "col", scatter_dimension=0, tiled=True
    ).astype(jnp.float32)


def sum_weight(partial_sum):
    return lax.psum_scatter(
        partial_sum.astype(jnp.bfloat16), "row", scatter_dimension=0, tiled=True
    )


def norm_apply(values, gain_vec):
    row_scale = lax.rsqrt(jnp.mean(values * values, axis=1) + EPS)
    return (values * row_scale[:, None] * gain_vec, row_scale)


def norm_back(values, row_scale, gain_vec, grads, width_all, total_fn):
    inner = total_fn(jnp.sum(grads * gain_vec * values, axis=1))
    d_values = (
        grads * gain_vec * row_scale[:, None] - values * (inner * row_scale**3 / width_all)[:, None]
    )
    d_gain = jnp.sum(grads * values * row_scale[:, None], axis=0)
    return (d_values, d_gain)


def causal_conv(signal, kernel):
    tap_count = kernel.shape[0]
    length = signal.shape[0]
    padded = jnp.concatenate(
        [jnp.zeros((tap_count - 1, signal.shape[1]), jnp.float32), signal], axis=0
    )
    result = kernel[tap_count - 1] * signal
    for offset in range(tap_count - 1):
        result = result + kernel[offset] * padded[offset : offset + length]
    return result


def per_channel(values, head_width):
    wide = jnp.broadcast_to(values[..., None], values.shape + (head_width,))
    return wide.reshape(values.shape[:-1] + (values.shape[-1] * head_width,))


def batch_dot(spec, left, right):
    return jnp.einsum(
        spec,
        left.astype(jnp.bfloat16),
        right.astype(jnp.bfloat16),
        preferred_element_type=jnp.float32,
    )


def state_space(step_decay, scaled_inner, b_matrix, c_matrix):
    length, heads = step_decay.shape
    width = scaled_inner.shape[1]
    head_width = width // heads
    chunks = length // CHUNK
    order = jnp.arange(CHUNK)
    causal = order[:, None] >= order[None, :]
    decay = jnp.einsum(
        "ts,csh->cth",
        causal.astype(jnp.float32),
        step_decay.reshape(chunks, CHUNK, heads),
        precision=HIGH,
    )
    whole = decay[:, -1]
    by_head = decay.transpose(0, 2, 1)
    spans = by_head[:, :, :, None] - by_head[:, :, None, :]
    mixing = jnp.where(causal, jnp.exp(jnp.where(causal, spans, 0.0)), 0.0)
    b_chunks = b_matrix.reshape(chunks, CHUNK, -1)
    c_chunks = c_matrix.reshape(chunks, CHUNK, -1)
    inner = scaled_inner.reshape(chunks, CHUNK, width)
    affinity = batch_dot("ctn,csn->cts", c_chunks, b_chunks)
    within = batch_dot(
        "chts,cshp->cthp",
        mixing * affinity[:, None],
        inner.reshape(chunks, CHUNK, heads, head_width),
    ).reshape(chunks, CHUNK, width)
    to_end = per_channel(jnp.exp(whole[:, None] - decay), head_width)
    added = batch_dot("csn,csq->cnq", b_chunks, inner * to_end)
    kept = per_channel(jnp.exp(whole), head_width)
    state = jnp.zeros_like(added[0])
    states = []
    for index in range(chunks):
        states.append(state)
        state = state * kept[index] + added[index]
    across = batch_dot("ctn,cnq->ctq", c_chunks, jnp.stack(states))
    across = across * per_channel(jnp.exp(decay), head_width)
    return (within + across).reshape(length, width)


def mixer_front(
    inputs, conv_inner, conv_state, step_bias, decay_log, skip_scale, key_pick, head_dim
):
    inner_width = conv_inner.shape[1]
    mamba_heads = step_bias.shape[0]
    head_width = inner_width // mamba_heads
    state_size = conv_state.shape[1] // 2
    query_width = key_pick.shape[0] * head_dim
    length = inputs.shape[0]
    gate_part = inputs[:, :inner_width]
    inner_part = inputs[:, inner_width : 2 * inner_width]
    first_col = 2 * inner_width
    step_part = inputs[:, first_col : first_col + mamba_heads]
    first_col = first_col + mamba_heads
    query_part = inputs[:, first_col : first_col + query_width]
    first_col = first_col + query_width
    state_part = inputs[:, first_col : first_col + 2 * state_size]
    keyval_part = inputs[:, first_col + 2 * state_size :]
    positions = jnp.arange(length)
    causal = positions[:, None] >= positions[None, :]
    mixed_inner = jax.nn.silu(causal_conv(inner_part, conv_inner))
    mixed_state = jax.nn.silu(causal_conv(state_part, conv_state))
    b_matrix = mixed_state[:, :state_size]
    c_matrix = mixed_state[:, state_size:]
    step_size = jax.nn.softplus(step_part + step_bias)
    ssm_out = state_space(
        step_size * -jnp.exp(decay_log),
        mixed_inner * per_channel(step_size, head_width),
        b_matrix,
        c_matrix,
    )
    ssm_out = ssm_out + per_channel(skip_scale, head_width) * mixed_inner
    gated = ssm_out * jax.nn.silu(gate_part)
    key_heads = keyval_part.shape[1] // (2 * head_dim)
    queries = query_part.reshape(length, -1, head_dim)
    keys_all = keyval_part[:, : key_heads * head_dim].reshape(length, key_heads, head_dim)
    values_all = keyval_part[:, key_heads * head_dim :].reshape(length, key_heads, head_dim)
    picked = (key_pick[:, None] == jnp.arange(key_heads)[None, :]).astype(jnp.float32)
    keys_used = batch_dot("hk,skd->shd", picked, keys_all)
    values_used = batch_dot("hk,skd->shd", picked, values_all)
    scores = batch_dot("thd,shd->hts", queries, keys_used) / math.sqrt(head_dim)
    scores = jnp.where(causal[None], scores, -1e30)
    peak = lax.stop_gradient(jnp.max(scores, axis=2, keepdims=True))
    weights = jnp.exp(scores - peak)
    weights = weights / jnp.sum(weights, axis=2, keepdims=True)
    attended = batch_dot("hts,shd->thd", weights, values_used).reshape(length, -1)
    return (gated, attended)


def on_device(
    tokens_in,
    gain_first,
    proj_gate,
    proj_inner,
    proj_step,
    proj_query,
    proj_state,
    proj_keyval,
    conv_inner,
    conv_state,
    step_bias,
    decay_log,
    skip_scale,
    mixer_gain,
    out_mamba,
    out_attn,
    gain_second,
    ffn_gate,
    ffn_up,
    ffn_down,
    out_grad,
):
    inner_local = proj_gate.shape[1]
    step_local = proj_step.shape[1]
    query_local = proj_query.shape[1]
    block_cols = 2 * inner_local + step_local + query_local
    state_cols = proj_state.shape[1]
    ffn_local = ffn_gate.shape[1]
    gain_local = gain_first.shape[0]
    heads_local = query_local // HD
    key_pick = (lax.axis_index("col") * heads_local + jnp.arange(heads_local)) // (HQ // HK)

    entering = lax.all_to_all(
        jnp.stack([tokens_in, out_grad]),
        ("row", "col"),
        split_axis=1,
        concat_axis=2,
        tiled=True,
    )
    gains = lax.all_gather(
        jnp.stack([gain_first, gain_second]), ("row", "col"), axis=1, tiled=True
    )
    kernel_in = gather_rows(
        jnp.concatenate(
            [proj_gate, proj_inner, proj_step, proj_query, proj_state, proj_keyval], axis=1
        )
    )
    kernel_out = gather_rows(jnp.concatenate([out_mamba, out_attn], axis=0).T)
    kernel_ffn = gather_rows(jnp.concatenate([ffn_gate, ffn_up, ffn_down.T], axis=1))
    kernel_gate_up = kernel_ffn[:, : 2 * ffn_local]
    kernel_down = kernel_ffn[:, 2 * ffn_local :]

    residual = entering[0].astype(jnp.float32)
    normed_one, scale_one = norm_apply(residual, gains[0])
    wide_one = gather_tokens(normed_one.astype(jnp.bfloat16))
    mixer_in = plain_dot(wide_one, kernel_in).astype(jnp.bfloat16)
    seq_count = mixer_in.shape[0] // SEQ_LEN

    def local_front(values, kernel_one, kernel_two, bias_vec, decay_vec, skip_vec):
        parts = [
            mixer_front(
                values[index * SEQ_LEN : (index + 1) * SEQ_LEN],
                kernel_one,
                kernel_two,
                bias_vec,
                decay_vec,
                skip_vec,
                key_pick,
                HD,
            )
            for index in range(seq_count)
        ]
        return tuple(jnp.concatenate(side, axis=0) for side in zip(*parts))

    (gated, attended), pull = jax.vjp(
        local_front,
        mixer_in.astype(jnp.float32),
        conv_inner,
        conv_state,
        step_bias,
        decay_log,
        skip_scale,
    )
    gated_scale = lax.rsqrt(lax.psum(jnp.sum(gated * gated, axis=1), "col") / DI + EPS)
    gated_norm = gated * gated_scale[:, None] * mixer_gain
    mixed = jnp.concatenate([gated_norm, attended], axis=1).astype(jnp.bfloat16)
    hidden = residual + sum_tokens(dot_nt(mixed, kernel_out))
    normed_two, scale_two = norm_apply(hidden, gains[1])
    wide_two = gather_tokens(normed_two.astype(jnp.bfloat16))
    out_wide = gather_tokens(entering[1])
    gate_up = plain_dot(wide_two, kernel_gate_up)
    gate_val = gate_up[:, :ffn_local]
    up_val = gate_up[:, ffn_local:]
    sigmoid_gate = jax.nn.sigmoid(gate_val)
    active = (gate_val * sigmoid_gate * up_val).astype(jnp.bfloat16)
    d_active = plain_dot(out_wide, kernel_down)
    d_gate = d_active * up_val * sigmoid_gate * (1.0 + gate_val * (1.0 - sigmoid_gate))
    d_up = d_active * gate_val * sigmoid_gate
    d_gate_up = jnp.concatenate([d_gate, d_up], axis=1).astype(jnp.bfloat16)
    d_normed_two = sum_tokens(dot_nt(d_gate_up, kernel_gate_up))
    ffn_part = sum_weight(
        jnp.concatenate([dot_tn(wide_two, d_gate_up), dot_tn(out_wide, active)], axis=1)
    )
    block_out = (hidden + sum_tokens(dot_nt(active, kernel_down))).astype(jnp.bfloat16)

    def whole_row(values):
        return values

    d_hidden_norm, grad_second = norm_back(
        hidden, scale_two, gains[1], d_normed_two, D, whole_row
    )
    d_hidden = entering[1].astype(jnp.float32) + d_hidden_norm
    hidden_wide = gather_tokens(d_hidden.astype(jnp.bfloat16))
    d_mixed = plain_dot(hidden_wide, kernel_out)
    d_gated, grad_gain_mix = norm_back(
        gated,
        gated_scale,
        mixer_gain,
        d_mixed[:, :inner_local],
        DI,
        lambda values: lax.psum(values, "col"),
    )
    mixer_grads = pull((d_gated, d_mixed[:, inner_local:]))
    d_mixer_in = mixer_grads[0].astype(jnp.bfloat16)
    d_normed_one = sum_tokens(dot_nt(d_mixer_in, kernel_in))
    d_tokens_norm, grad_first = norm_back(
        residual, scale_one, gains[0], d_normed_one, D, whole_row
    )
    grad_tokens = (d_hidden + d_tokens_norm).astype(jnp.bfloat16)
    leaving = lax.all_to_all(
        jnp.stack([block_out, grad_tokens]),
        ("row", "col"),
        split_axis=2,
        concat_axis=1,
        tiled=True,
    )
    out_part = sum_weight(dot_tn(hidden_wide, mixed))
    in_part = sum_weight(dot_tn(wide_one, d_mixer_in))
    own_cols = 3 * ffn_local + out_part.shape[1]
    own_sum = lax.psum(
        jnp.concatenate([ffn_part, out_part, in_part[:, :block_cols]], axis=1), "dp"
    ).astype(jnp.float32)
    shared_sum = lax.psum(in_part[:, block_cols:], ("dp", "col")).astype(jnp.float32)
    gate_up_sum = own_sum[:, : 2 * ffn_local]
    down_sum = own_sum[:, 2 * ffn_local : 3 * ffn_local].T
    outer_sum = own_sum[:, 3 * ffn_local : own_cols].T
    block_sum = own_sum[:, own_cols:]
    conv_sum, bias_sum, decay_sum, skip_sum, mixer_sum = lax.psum(
        (mixer_grads[1], mixer_grads[3], mixer_grads[4], mixer_grads[5], grad_gain_mix),
        ("dp", "row"),
    )
    state_sum, first_all, second_all = lax.psum(
        (mixer_grads[2], grad_first, grad_second), ("dp", "row", "col")
    )
    gain_at = lax.axis_index(("row", "col")) * gain_local
    first_sum = lax.dynamic_slice(first_all, (gain_at,), (gain_local,))
    second_sum = lax.dynamic_slice(second_all, (gain_at,), (gain_local,))
    first_col = 2 * inner_local
    return (
        leaving[0],
        leaving[1],
        first_sum,
        block_sum[:, :inner_local],
        block_sum[:, inner_local:first_col],
        block_sum[:, first_col : first_col + step_local],
        block_sum[:, first_col + step_local :],
        shared_sum[:, :state_cols],
        shared_sum[:, state_cols:],
        conv_sum,
        state_sum,
        bias_sum,
        decay_sum,
        skip_sum,
        mixer_sum,
        outer_sum[:inner_local],
        outer_sum[inner_local:],
        second_sum,
        gate_up_sum[:, :ffn_local],
        gate_up_sum[:, ffn_local:],
        down_sum,
    )


def solution(mesh):
    in_specs = (
        P("dp", ("row", "col")),
        P(("row", "col")),
        P("row", "col"),
        P("row", "col"),
        P("row", "col"),
        P("row", "col"),
        P("row", None),
        P("row", None),
        P(None, "col"),
        P(),
        P("col"),
        P("col"),
        P("col"),
        P("col"),
        P("col", "row"),
        P("col", "row"),
        P(("row", "col")),
        P("row", "col"),
        P("row", "col"),
        P("col", "row"),
        P("dp", ("row", "col")),
    )
    out_specs = (
        P("dp", ("row", "col")),
        P("dp", ("row", "col")),
        P(("row", "col")),
        P("row", "col"),
        P("row", "col"),
        P("row", "col"),
        P("row", "col"),
        P("row", None),
        P("row", None),
        P(None, "col"),
        P(),
        P("col"),
        P("col"),
        P("col"),
        P("col"),
        P("col", "row"),
        P("col", "row"),
        P(("row", "col")),
        P("row", "col"),
        P("row", "col"),
        P("col", "row"),
    )
    return jax.shard_map(
        on_device, mesh=mesh, in_specs=in_specs, out_specs=out_specs, check_vma=False
    )
```

```python
import math

import jax
import jax.numpy as jnp
from jax import lax
from jax.sharding import PartitionSpec as P

D = 1024
HQ = 8
HK = 2
HD = 64
DI = 1536
SEQ_LEN = 1024
CHUNK = 128


EPS = 1e-06
HIGH = lax.Precision.HIGHEST


def plain_dot(left, right):
    return jnp.dot(left, right, preferred_element_type=jnp.float32)


def dot_nt(left, right):
    return lax.dot_general(
        left, right, (((1,), (1,)), ((), ())), preferred_element_type=jnp.float32
    )


def dot_tn(left, right):
    return lax.dot_general(
        left, right, (((0,), (0,)), ((), ())), preferred_element_type=jnp.float32
    )


def gather_rows(weight):
    return lax.all_gather(weight, "row", axis=0, tiled=True)


def gather_tokens(values):
    return lax.all_gather(values, "col", axis=0, tiled=True)


def sum_tokens(partial_sum):
    return lax.psum_scatter(
        partial_sum.astype(jnp.bfloat16), "col", scatter_dimension=0, tiled=True
    ).astype(jnp.float32)


def sum_weight(partial_sum):
    return lax.psum_scatter(
        partial_sum.astype(jnp.bfloat16), "row", scatter_dimension=0, tiled=True
    )


def norm_apply(values, gain_vec):
    row_scale = lax.rsqrt(jnp.mean(values * values, axis=1) + EPS)
    return (values * row_scale[:, None] * gain_vec, row_scale)


def norm_back(values, row_scale, gain_vec, grads, width_all, total_fn):
    inner = total_fn(jnp.sum(grads * gain_vec * values, axis=1))
    d_values = (
        grads * gain_vec * row_scale[:, None] - values * (inner * row_scale**3 / width_all)[:, None]
    )
    d_gain = jnp.sum(grads * values * row_scale[:, None], axis=0)
    return (d_values, d_gain)


def causal_conv(signal, kernel):
    tap_count = kernel.shape[0]
    length = signal.shape[0]
    padded = jnp.concatenate(
        [jnp.zeros((tap_count - 1, signal.shape[1]), jnp.float32), signal], axis=0
    )
    result = kernel[tap_count - 1] * signal
    for offset in range(tap_count - 1):
        result = result + kernel[offset] * padded[offset : offset + length]
    return result


def per_channel(values, head_width):
    wide = jnp.broadcast_to(values[..., None], values.shape + (head_width,))
    return wide.reshape(values.shape[:-1] + (values.shape[-1] * head_width,))


def batch_dot(spec, left, right):
    return jnp.einsum(
        spec,
        left.astype(jnp.bfloat16),
        right.astype(jnp.bfloat16),
        preferred_element_type=jnp.float32,
    )


def state_space(step_decay, scaled_inner, b_matrix, c_matrix):
    length, heads = step_decay.shape
    width = scaled_inner.shape[1]
    head_width = width // heads
    chunks = length // CHUNK
    order = jnp.arange(CHUNK)
    causal = order[:, None] >= order[None, :]
    decay = jnp.einsum(
        "ts,csh->cth",
        causal.astype(jnp.float32),
        step_decay.reshape(chunks, CHUNK, heads),
        precision=HIGH,
    )
    whole = decay[:, -1]
    by_head = decay.transpose(0, 2, 1)
    spans = by_head[:, :, :, None] - by_head[:, :, None, :]
    mixing = jnp.where(causal, jnp.exp(jnp.where(causal, spans, 0.0)), 0.0)
    b_chunks = b_matrix.reshape(chunks, CHUNK, -1)
    c_chunks = c_matrix.reshape(chunks, CHUNK, -1)
    inner = scaled_inner.reshape(chunks, CHUNK, width)
    affinity = batch_dot("ctn,csn->cts", c_chunks, b_chunks)
    within = batch_dot(
        "chts,cshp->cthp",
        mixing * affinity[:, None],
        inner.reshape(chunks, CHUNK, heads, head_width),
    ).reshape(chunks, CHUNK, width)
    to_end = per_channel(jnp.exp(whole[:, None] - decay), head_width)
    added = batch_dot("csn,csq->cnq", b_chunks, inner * to_end)
    kept = per_channel(jnp.exp(whole), head_width)
    state = jnp.zeros_like(added[0])
    states = []
    for index in range(chunks):
        states.append(state)
        state = state * kept[index] + added[index]
    across = batch_dot("ctn,cnq->ctq", c_chunks, jnp.stack(states))
    across = across * per_channel(jnp.exp(decay), head_width)
    return (within + across).reshape(length, width)


def mixer_front(
    inputs, conv_inner, conv_state, step_bias, decay_log, skip_scale, key_pick, head_dim
):
    inner_width = conv_inner.shape[1]
    mamba_heads = step_bias.shape[0]
    head_width = inner_width // mamba_heads
    state_size = conv_state.shape[1] // 2
    query_width = key_pick.shape[0] * head_dim
    length = inputs.shape[0]
    gate_part = inputs[:, :inner_width]
    inner_part = inputs[:, inner_width : 2 * inner_width]
    first_col = 2 * inner_width
    step_part = inputs[:, first_col : first_col + mamba_heads]
    first_col = first_col + mamba_heads
    query_part = inputs[:, first_col : first_col + query_width]
    first_col = first_col + query_width
    state_part = inputs[:, first_col : first_col + 2 * state_size]
    keyval_part = inputs[:, first_col + 2 * state_size :]
    positions = jnp.arange(length)
    causal = positions[:, None] >= positions[None, :]
    mixed_inner = jax.nn.silu(causal_conv(inner_part, conv_inner))
    mixed_state = jax.nn.silu(causal_conv(state_part, conv_state))
    b_matrix = mixed_state[:, :state_size]
    c_matrix = mixed_state[:, state_size:]
    step_size = jax.nn.softplus(step_part + step_bias)
    ssm_out = state_space(
        step_size * -jnp.exp(decay_log),
        mixed_inner * per_channel(step_size, head_width),
        b_matrix,
        c_matrix,
    )
    ssm_out = ssm_out + per_channel(skip_scale, head_width) * mixed_inner
    gated = ssm_out * jax.nn.silu(gate_part)
    key_heads = keyval_part.shape[1] // (2 * head_dim)
    queries = query_part.reshape(length, -1, head_dim)
    keys_all = keyval_part[:, : key_heads * head_dim].reshape(length, key_heads, head_dim)
    values_all = keyval_part[:, key_heads * head_dim :].reshape(length, key_heads, head_dim)
    picked = (key_pick[:, None] == jnp.arange(key_heads)[None, :]).astype(jnp.float32)
    keys_used = batch_dot("hk,skd->shd", picked, keys_all)
    values_used = batch_dot("hk,skd->shd", picked, values_all)
    scores = batch_dot("thd,shd->hts", queries, keys_used) / math.sqrt(head_dim)
    scores = jnp.where(causal[None], scores, -1e30)
    peak = lax.stop_gradient(jnp.max(scores, axis=2, keepdims=True))
    weights = jnp.exp(scores - peak)
    weights = weights / jnp.sum(weights, axis=2, keepdims=True)
    attended = batch_dot("hts,shd->thd", weights, values_used).reshape(length, -1)
    return (gated, attended)


def on_device(
    tokens_in,
    gain_first,
    proj_gate,
    proj_inner,
    proj_step,
    proj_query,
    proj_state,
    proj_keyval,
    conv_inner,
    conv_state,
    step_bias,
    decay_log,
    skip_scale,
    mixer_gain,
    out_mamba,
    out_attn,
    gain_second,
    ffn_gate,
    ffn_up,
    ffn_down,
    out_grad,
):
    inner_local = proj_gate.shape[1]
    step_local = proj_step.shape[1]
    query_local = proj_query.shape[1]
    block_cols = 2 * inner_local + step_local + query_local
    state_cols = proj_state.shape[1]
    ffn_local = ffn_gate.shape[1]
    gain_local = gain_first.shape[0]
    heads_local = query_local // HD
    key_pick = (lax.axis_index("col") * heads_local + jnp.arange(heads_local)) // (HQ // HK)

    entering = lax.all_to_all(
        jnp.stack([tokens_in, out_grad]),
        ("row", "col"),
        split_axis=1,
        concat_axis=2,
        tiled=True,
    )
    gains = lax.all_gather(
        jnp.stack([gain_first, gain_second]), ("row", "col"), axis=1, tiled=True
    )
    kernel_in = gather_rows(
        jnp.concatenate(
            [proj_gate, proj_inner, proj_step, proj_query, proj_state, proj_keyval], axis=1
        )
    )
    kernel_out = gather_rows(jnp.concatenate([out_mamba, out_attn], axis=0).T)

    residual = entering[0].astype(jnp.float32)
    normed_one, scale_one = norm_apply(residual, gains[0])
    wide_one = gather_tokens(normed_one.astype(jnp.bfloat16))
    ffn_block, wide_one = lax.optimization_barrier(
        (jnp.concatenate([ffn_gate, ffn_up, ffn_down.T], axis=1), wide_one)
    )
    kernel_ffn = gather_rows(ffn_block)
    mixer_in = plain_dot(wide_one, kernel_in).astype(jnp.bfloat16)
    seq_count = mixer_in.shape[0] // SEQ_LEN

    def local_front(values, kernel_one, kernel_two, bias_vec, decay_vec, skip_vec):
        parts = [
            mixer_front(
                values[index * SEQ_LEN : (index + 1) * SEQ_LEN],
                kernel_one,
                kernel_two,
                bias_vec,
                decay_vec,
                skip_vec,
                key_pick,
                HD,
            )
            for index in range(seq_count)
        ]
        return tuple(jnp.concatenate(side, axis=0) for side in zip(*parts))

    (gated, attended), pull = jax.vjp(
        local_front,
        mixer_in.astype(jnp.float32),
        conv_inner,
        conv_state,
        step_bias,
        decay_log,
        skip_scale,
    )
    gated_scale = lax.rsqrt(lax.psum(jnp.sum(gated * gated, axis=1), "col") / DI + EPS)
    gated_norm = gated * gated_scale[:, None] * mixer_gain
    mixed = jnp.concatenate([gated_norm, attended], axis=1).astype(jnp.bfloat16)
    mixed, kernel_ffn = lax.optimization_barrier((mixed, kernel_ffn))
    kernel_gate_up = kernel_ffn[:, : 2 * ffn_local]
    kernel_down = kernel_ffn[:, 2 * ffn_local :]
    hidden = residual + sum_tokens(dot_nt(mixed, kernel_out))
    normed_two, scale_two = norm_apply(hidden, gains[1])
    wide_two = gather_tokens(normed_two.astype(jnp.bfloat16))
    out_wide = gather_tokens(entering[1])
    gate_up = plain_dot(wide_two, kernel_gate_up)
    gate_val = gate_up[:, :ffn_local]
    up_val = gate_up[:, ffn_local:]
    sigmoid_gate = jax.nn.sigmoid(gate_val)
    active = (gate_val * sigmoid_gate * up_val).astype(jnp.bfloat16)
    d_active = plain_dot(out_wide, kernel_down)
    d_gate = d_active * up_val * sigmoid_gate * (1.0 + gate_val * (1.0 - sigmoid_gate))
    d_up = d_active * gate_val * sigmoid_gate
    d_gate_up = jnp.concatenate([d_gate, d_up], axis=1).astype(jnp.bfloat16)
    d_normed_two = sum_tokens(dot_nt(d_gate_up, kernel_gate_up))
    ffn_grads = jnp.concatenate(
        [dot_tn(wide_two, d_gate_up), dot_tn(out_wide, active)], axis=1
    ).astype(jnp.bfloat16)
    block_partial = dot_nt(active, kernel_down).astype(jnp.bfloat16)

    def whole_row(values):
        return values

    d_hidden_norm, grad_second = norm_back(
        hidden, scale_two, gains[1], d_normed_two, D, whole_row
    )
    d_hidden = entering[1].astype(jnp.float32) + d_hidden_norm
    hidden_wide = gather_tokens(d_hidden.astype(jnp.bfloat16))
    ffn_grads, block_partial, hidden_wide = lax.optimization_barrier(
        (ffn_grads, block_partial, hidden_wide)
    )
    d_mixed = plain_dot(hidden_wide, kernel_out)
    block_out = (hidden + sum_tokens(block_partial)).astype(jnp.bfloat16)
    ffn_part = sum_weight(ffn_grads)
    out_part = sum_weight(dot_tn(hidden_wide, mixed))
    d_gated, grad_gain_mix = norm_back(
        gated,
        gated_scale,
        mixer_gain,
        d_mixed[:, :inner_local],
        DI,
        lambda values: lax.psum(values, "col"),
    )
    mixer_grads = pull((d_gated, d_mixed[:, inner_local:]))
    d_mixer_in, block_out, ffn_part, out_part = lax.optimization_barrier(
        (mixer_grads[0].astype(jnp.bfloat16), block_out, ffn_part, out_part)
    )
    d_normed_one = sum_tokens(dot_nt(d_mixer_in, kernel_in))
    d_tokens_norm, grad_first = norm_back(
        residual, scale_one, gains[0], d_normed_one, D, whole_row
    )
    grad_tokens = (d_hidden + d_tokens_norm).astype(jnp.bfloat16)
    leaving = lax.all_to_all(
        jnp.stack([block_out, grad_tokens]),
        ("row", "col"),
        split_axis=2,
        concat_axis=1,
        tiled=True,
    )
    in_part = sum_weight(dot_tn(wide_one, d_mixer_in))
    own_sum = lax.psum(jnp.concatenate([ffn_part, out_part], axis=1), "dp").astype(jnp.float32)
    block_sum = lax.psum(in_part[:, :block_cols], "dp").astype(jnp.float32)
    shared_sum = lax.psum(in_part[:, block_cols:], ("dp", "col")).astype(jnp.float32)
    gate_up_sum = own_sum[:, : 2 * ffn_local]
    down_sum = own_sum[:, 2 * ffn_local : 3 * ffn_local].T
    outer_sum = own_sum[:, 3 * ffn_local :].T
    col_count = lax.axis_size("col")
    col_at = lax.axis_index("col")
    own_small = jnp.concatenate(
        [
            mixer_grads[1].reshape(-1),
            mixer_grads[3],
            mixer_grads[4],
            mixer_grads[5],
            grad_gain_mix,
        ]
    )
    slots = jnp.where(jnp.arange(col_count)[:, None] == col_at, own_small[None, :], 0.0)
    small = lax.psum(
        jnp.concatenate(
            [slots.reshape(-1), mixer_grads[2].reshape(-1), grad_first, grad_second]
        ),
        ("dp", "row", "col"),
    )
    own_size = own_small.shape[0]
    own_all = lax.dynamic_slice(small, (col_at * own_size,), (own_size,))
    cuts = [conv_inner.size]
    for count in (step_local, step_local, step_local):
        cuts.append(cuts[-1] + count)
    conv_sum, bias_sum, decay_sum, skip_sum, mixer_sum = jnp.split(own_all, cuts)
    conv_sum = conv_sum.reshape(conv_inner.shape)
    rest = small[col_count * own_size :]
    state_sum = rest[: conv_state.size].reshape(conv_state.shape)
    first_all = rest[conv_state.size : conv_state.size + D]
    second_all = rest[conv_state.size + D :]
    gain_at = lax.axis_index(("row", "col")) * gain_local
    first_sum = lax.dynamic_slice(first_all, (gain_at,), (gain_local,))
    second_sum = lax.dynamic_slice(second_all, (gain_at,), (gain_local,))
    first_col = 2 * inner_local
    return (
        leaving[0],
        leaving[1],
        first_sum,
        block_sum[:, :inner_local],
        block_sum[:, inner_local:first_col],
        block_sum[:, first_col : first_col + step_local],
        block_sum[:, first_col + step_local :],
        shared_sum[:, :state_cols],
        shared_sum[:, state_cols:],
        conv_sum,
        state_sum,
        bias_sum,
        decay_sum,
        skip_sum,
        mixer_sum,
        outer_sum[:inner_local],
        outer_sum[inner_local:],
        second_sum,
        gate_up_sum[:, :ffn_local],
        gate_up_sum[:, ffn_local:],
        down_sum,
    )


def solution(mesh):
    in_specs = (
        P("dp", ("row", "col")),
        P(("row", "col")),
        P("row", "col"),
        P("row", "col"),
        P("row", "col"),
        P("row", "col"),
        P("row", None),
        P("row", None),
        P(None, "col"),
        P(),
        P("col"),
        P("col"),
        P("col"),
        P("col"),
        P("col", "row"),
        P("col", "row"),
        P(("row", "col")),
        P("row", "col"),
        P("row", "col"),
        P("col", "row"),
        P("dp", ("row", "col")),
    )
    out_specs = (
        P("dp", ("row", "col")),
        P("dp", ("row", "col")),
        P(("row", "col")),
        P("row", "col"),
        P("row", "col"),
        P("row", "col"),
        P("row", "col"),
        P("row", None),
        P("row", None),
        P(None, "col"),
        P(),
        P("col"),
        P("col"),
        P("col"),
        P("col"),
        P("col", "row"),
        P("col", "row"),
        P(("row", "col")),
        P("row", "col"),
        P("row", "col"),
        P("col", "row"),
    )
    return jax.shard_map(
        on_device, mesh=mesh, in_specs=in_specs, out_specs=out_specs, check_vma=False
    )
```
